32 devices in a mesh: ctx: 2 (over core), exp: 16 (over z, y, x).
Axes of the slice: x: 2, y: 2, z: 4, core: 2. Of those that a mesh axis runs over, the one named last changes fastest.
Arguments:
- queries: bfloat16 [1024, 4096], P('ctx', 'exp'), may hold values from -32 to 32
- keys: bfloat16 [1024, 4096], P('ctx', 'exp'), may hold values from -4 to 4
- values: bfloat16 [1024, 4096], P('ctx', 'exp'), may hold values from -6 to 6
- out_proj: bfloat16 [4096, 3584], P('exp'), may hold values from -0.5 to 0.5
- residual: bfloat16 [1024, 3584], P(('ctx', 'exp')), may hold values from -6 to 6
- norm_gain: float32 [3584], replicated, may hold values from 0.25 to 1.75
- routes: int32 [1024, 8], P(('ctx', 'exp')), may hold values from 0 to 15, all different within a row; in each aligned block of 32 rows (0 to 31, 32 to 63, ...) at most 20 rows name the same one
- combine: float32 [1024, 8], P(('ctx', 'exp')), may hold values from 0.1 to 0.5
- w_gate: bfloat16 [16, 3584, 1024], P('exp', None, 'ctx'), may hold values from -0.09375 to 0.09375
- w_up: bfloat16 [16, 3584, 1024], P('exp', None, 'ctx'), may hold values from -0.09375 to 0.09375
- w_down: bfloat16 [16, 1024, 3584], P('exp', 'ctx'), may hold values from -0.1875 to 0.1875
Outputs:
- layer_out: bfloat16 [1024, 3584], P(('ctx', 'exp'))
The draws below stay inside these ranges and needn't reach their ends.
Inputs may be any that keep to these rules, and one draw needn't show every extreme that they name: `routes`: each row names 8 different experts. Within each aligned block of 32 rows no expert is named by more than 20 rows, and some block names some expert exactly 20 times.
All inputs are finite; a program needn't handle non-finite values.
Results may differ from the reference program's by a relative error of at most 0.023.
Values may be sent and summed in bfloat16 or wider, within the bound.
A program may use at most 128 MiB of HBM per device.

```python
import math
import jax
import jax.numpy as jnp
import numpy as np
from jax import lax

D = 3584
FF = 1024
HD = 128
H_DEV = 2
TOP = 8
TOK_DEV = 32
HEADS = 32
EXPERTS = 16
MOST = 20
SEQ = 1024
N_CTX = 2
N_EXP = 16


def base_keys(key):
    sub_key = jax.random.fold_in(key, 11)
    table = jnp.clip(jax.random.normal(sub_key, (SEQ, HEADS * HD), jnp.float32), -4.0, 4.0)
    return table


def draw_keys(key, part):
    return base_keys(key).astype(jnp.bfloat16)


def draw_queries(key, part):
    sub_key = jax.random.fold_in(key, 23)
    table = jnp.clip(jax.random.normal(sub_key, (SEQ, HEADS * HD), jnp.float32), -4.0, 4.0)
    return table.astype(jnp.bfloat16)


def block_scale(key, dims, shards, least, largest):
    level = 1.0
    for position, parts in shards:
        steps = jax.random.uniform(jax.random.fold_in(jax.random.fold_in(key, 6), position), (parts,), jnp.float32, least / len(shards), largest / len(shards))
        level = level * jnp.repeat(jnp.exp(steps), dims[position] // parts).reshape((-1,) + (1,) * (len(dims) - 1 - position))
    return level


def deal_out(stream_key, own, number, rows, number_of, top, reach, lean):
    sequence = jax.random.permutation(stream_key, number_of)
    crowded, common = portions_of(number_of, rows * top, reach, lean, True), portions_of(number_of, rows * top, reach, lean, False)
    places = jnp.arange(number_of)

    def named(lengths, turn):
        used = int((lengths > 0).sum())
        fixed = max(1, used // 4)
        moved = fixed + (places - fixed + turn * (used - fixed)) % max(1, number_of - fixed)
        return jnp.zeros((number_of,), jnp.int32).at[sequence[jnp.where(places < fixed, places, moved)]].set(jnp.asarray(lengths, jnp.int32))

    lengths = jnp.where(number % 4 == 0, named(crowded, number // 4), named(common, number - number // 4 - 1))
    mixed = jax.random.permutation(jax.random.fold_in(own, 3), number_of)
    source_of, receiver = mixed[0:number_of // 2 * 2:2], mixed[1:number_of // 2 * 2:2]
    room = jnp.minimum(lengths[source_of] - 1, reach - lengths[receiver]) // 2
    room = jnp.where((source_of == sequence[0]) | (receiver == sequence[0]) | (lengths[receiver] == 0), 0, jnp.maximum(room, 0))
    moved = jax.random.randint(jax.random.fold_in(own, 4), (number_of // 2,), 0, 1 << 20) % (room + 1)
    lengths = lengths.at[source_of].add(-moved).at[receiver].add(moved)
    items = jnp.searchsorted(jnp.cumsum(lengths), jnp.arange(rows * top), side="right").astype(jnp.int32)
    listing = items.reshape(top, rows).T
    listing = listing[jax.random.permutation(jax.random.fold_in(own, 1), rows)]
    turn = jax.random.randint(jax.random.fold_in(own, 2), (rows, 1), 0, top)
    return jnp.take_along_axis(listing, (jnp.arange(top)[None, :] + turn) % top, axis=1)


def portions_of(amount, total, reach, slope, full):
    weights = [(1 << 20) // math.isqrt(rank ** slope) + 1 for rank in range(1, amount + 1)]
    largest = reach if full else min(reach, max(-(-total // amount), total * weights[0] // sum(weights)))
    least = 1 if total - largest >= amount - 1 else 0
    holding, surplus = [largest] + [least] * (amount - 1), total - largest - least * (amount - 1)
    while surplus > 0:
        movable = [i for i in range(1, amount) if holding[i] < largest] or [i for i in range(1, amount) if holding[i] < reach]
        whole, left = sum([weights[i] for i in movable]), surplus
        for i in movable:
            more = min(reach - holding[i], max(1, left * weights[i] // whole), surplus)
            holding[i] = holding[i] + more
            surplus = surplus - more
    return np.array(holding)


def centred(key, extent, width, bound, shards=(), held_as=jnp.bfloat16):
    entries = jax.random.normal(key, extent, jnp.float32) * width
    if len(shards) > 0:
        entries = block_scale(key, extent, shards, -0.22, 0.18) * entries
    return jnp.clip(entries, min=-bound, max=bound).astype(held_as)


def setup_inputs(seed: int = 0) -> dict:
    key_list = jax.random.split(jax.random.key(seed), 12)
    queries = draw_queries(jax.random.fold_in(key_list[11], 71), 0)
    keys = draw_keys(jax.random.fold_in(key_list[11], 71), 0)
    values = centred(key_list[2], (SEQ, HEADS * HD), 1.0, 6.0, ((0, 2), (1, 16)))
    out_proj = centred(key_list[3], (HEADS * HD, D), HD ** -0.5, 0.5, ((0, 16),))
    residual = centred(key_list[4], (SEQ, D), 1.0, 6.0, ((0, 32),))
    norm_gain = jnp.clip(1.0 + 0.15 * jax.random.normal(key_list[5], (D,), jnp.float32), 0.25, 1.75)
    routes_keys = jax.random.split(jax.random.fold_in(key_list[6], 1), SEQ // TOK_DEV)
    routes_turns = jax.random.permutation(jax.random.fold_in(key_list[6], 3), SEQ // TOK_DEV)
    routes = jax.vmap(lambda own, number: deal_out(jax.random.fold_in(key_list[6], 2), own, number, TOK_DEV, EXPERTS, TOP, MOST, 2))(routes_keys, routes_turns).reshape((SEQ, TOP))
    combine = jnp.clip(0.1 + 0.4 * jax.random.uniform(key_list[7], (SEQ, TOP), jnp.float32) ** block_scale(key_list[7], (SEQ, TOP), ((0, 32),), -0.2, 0.2), 0.1, 0.5)
    w_gate = centred(key_list[8], (EXPERTS, D, FF), D ** -0.5, 0.09375, ((0, 16), (2, 2)))
    w_up = centred(key_list[9], (EXPERTS, D, FF), D ** -0.5, 0.09375, ((0, 16), (2, 2)))
    w_down = centred(key_list[10], (EXPERTS, FF, D), FF ** -0.5, 0.1875, ((0, 16), (1, 2)))
    return dict(queries=queries, keys=keys, values=values, out_proj=out_proj, residual=residual, norm_gain=norm_gain, routes=routes, combine=combine, w_gate=w_gate, w_up=w_up, w_down=w_down)


masked_score = -1e+30
norm_eps = 1e-06

def reference(queries, keys, values, out_proj, residual, norm_gain, routes, combine, w_gate, w_up, w_down):
    scaling = 1.0 / math.sqrt(HD)
    query_heads = queries.reshape(SEQ, HEADS, HD).transpose(1, 0, 2)
    key_heads = keys.reshape(SEQ, HEADS, HD).transpose(1, 0, 2)
    value_heads = values.reshape(SEQ, HEADS, HD).transpose(1, 0, 2)
    positions = jnp.arange(SEQ)
    causal_mask = positions[:, None] >= positions[None, :]

    def one_head(triple):
        query_one, key_one, value_one = triple
        scores = jnp.dot(query_one, key_one.T, preferred_element_type=jnp.float32) * scaling
        scores = jnp.where(causal_mask, scores, masked_score)
        peak = lax.optimization_barrier(jnp.max(scores, axis=1, keepdims=True))
        expo = jnp.exp(scores - peak)
        probs = expo.astype(jnp.bfloat16)
        summed = jnp.dot(probs, value_one, preferred_element_type=jnp.float32)
        return (summed / lax.optimization_barrier(jnp.sum(expo, axis=1, keepdims=True))).astype(jnp.bfloat16)
    head_outs = lax.map(one_head, (query_heads, key_heads, value_heads))
    attended = head_outs.transpose(1, 0, 2).reshape(SEQ, HEADS * HD)
    group_width = H_DEV * HD

    def add_group(group, total):
        cols = lax.dynamic_slice_in_dim(attended, group * group_width, group_width, 1)
        rows = lax.dynamic_slice_in_dim(out_proj, group * group_width, group_width, 0)
        term = jnp.dot(cols, rows, preferred_element_type=jnp.float32)
        term = lax.optimization_barrier(term.astype(jnp.bfloat16)).astype(jnp.float32)
        return total + term
    mixed = lax.fori_loop(0, N_EXP, add_group, jnp.zeros((SEQ, D), jnp.float32))
    stream = residual.astype(jnp.float32) + mixed
    normed = (stream * lax.rsqrt(lax.optimization_barrier(jnp.mean(stream * stream, axis=1, keepdims=True)) + norm_eps) * norm_gain).astype(jnp.bfloat16)
    block_count = SEQ // TOK_DEV
    pair_count = TOK_DEV * TOP
    flat_routes = routes.reshape(block_count, pair_count).astype(jnp.int32)
    expert_hot = (flat_routes[:, :, None] == jnp.arange(EXPERTS).astype(jnp.int32)[None, None, :]).astype(jnp.int32)
    earlier = jnp.cumsum(expert_hot, axis=1).astype(jnp.int32) - expert_hot
    slot_index = lax.optimization_barrier(jnp.sum(earlier * expert_hot, axis=2)).astype(jnp.int32)
    block_index = jnp.broadcast_to(jnp.arange(block_count).astype(jnp.int32)[:, None], (block_count, pair_count))
    token_index = block_index * TOK_DEV + (jnp.arange(pair_count).astype(jnp.int32) // TOP)[None, :]
    token_rows = normed[token_index]
    buffer = jnp.zeros((EXPERTS, block_count, MOST, D), jnp.bfloat16)
    buffer = buffer.at[flat_routes, block_index, slot_index].set(token_rows)
    quarter = FF // N_CTX

    def one_expert(group):
        expert_rows, gate_weight, up_weight, down_weight = group
        row_block = expert_rows.reshape(block_count * MOST, D)
        gate = jnp.dot(row_block, gate_weight, preferred_element_type=jnp.float32)
        upper = jnp.dot(row_block, up_weight, preferred_element_type=jnp.float32)
        act = (jax.nn.silu(gate) * upper).astype(jnp.bfloat16)
        total = jnp.zeros((block_count * MOST, D), jnp.float32)
        for part_index in range(N_CTX):
            part = jnp.dot(act[:, part_index * quarter:(part_index + 1) * quarter], down_weight[part_index * quarter:(part_index + 1) * quarter], preferred_element_type=jnp.float32)
            part = lax.optimization_barrier(part.astype(jnp.bfloat16)).astype(jnp.float32)
            total = total + part
        return total.astype(jnp.bfloat16).reshape(block_count, MOST, D)
    expert_out = lax.map(one_expert, (buffer, w_gate, w_up, w_down))
    picked = expert_out[flat_routes, block_index, slot_index].astype(jnp.float32)
    weighted = picked * combine.reshape(block_count, pair_count)[:, :, None]
    moe_sum = lax.optimization_barrier(jnp.sum(weighted.reshape(block_count, TOK_DEV, TOP, D), axis=2)).reshape(SEQ, D)
    return (stream + moe_sum).astype(jnp.bfloat16)
```

```python
import functools
import math

import jax
import jax.numpy as jnp
from jax import lax
from jax.experimental import pallas as pl
from jax.experimental.pallas import tpu as pltpu
from jax.sharding import PartitionSpec as P

HD = 128
LANES = 128
CHUNKS = 4
VMEM_BUDGET = 58 * 1024 * 1024


masked_score = -1e30
norm_eps = 1e-06


def exp_grid(experts):
    fast = 2 if experts % 2 == 0 else 1
    slow = 4 if (experts // fast) % 4 == 0 else 1
    return slow, experts // (fast * slow), fast


def layer_kernel(
    sizes,
    attended_ref,
    proj_ref,
    residual_ref,
    gain_ref,
    weigh_ref,
    gate_hbm,
    up_hbm,
    down_hbm,
    out_ref,
    term,
    mix_one,
    mix_two,
    mix_last,
    stream,
    tokens,
    weights,
    gate_w,
    up_w,
    down_w,
    gate,
    upper,
    act,
    parts,
    sum_ctx,
    sum_one,
    sum_two,
    sum_last,
    mix_send,
    mix_recv,
    tok_send,
    tok_recv,
    sum_send,
    sum_recv,
    load_sem,
):
    rows, width = residual_ref.shape
    chunks = term.shape[0]
    cols = width // chunks
    where_exp = lax.axis_index("exp")
    block = sizes["y"] * sizes["x"]
    coords = {
        "c": lax.axis_index("ctx"),
        "z": lax.div(where_exp, block),
        "y": lax.rem(lax.div(where_exp, sizes["x"]), sizes["y"]),
        "x": lax.rem(where_exp, sizes["x"]),
    }

    def peer(axis, ahead):
        there = dict(coords)
        there[axis] = lax.rem(coords[axis] + ahead, sizes[axis])
        number = (there["z"] * sizes["y"] + there["y"]) * sizes["x"] + there["x"]
        return (there["c"], number), there[axis]

    loads = [
        pltpu.make_async_copy(source, target, load_sem.at[i])
        for i, (source, target) in enumerate(
            ((gate_hbm, gate_w), (up_hbm, up_w), (down_hbm, down_w))
        )
    ]
    for load in loads:
        load.start()

    barrier = pltpu.get_barrier_semaphore()
    greeted = 0
    for axis in ("c", "z", "y", "x"):
        for ahead in range(1, sizes[axis]):
            device, _ = peer(axis, ahead)
            pl.semaphore_signal(
                barrier, inc=1, device_id=device, device_id_type=pl.DeviceIdType.MESH
            )
            greeted += 1
    pl.semaphore_wait(barrier, greeted)

    pending = []

    def remote(source, target, send_sem, recv_sem, device):
        copy = pltpu.make_async_remote_copy(
            src_ref=source,
            dst_ref=target,
            send_sem=send_sem,
            recv_sem=recv_sem,
            device_id=device,
            device_id_type=pl.DeviceIdType.MESH,
        )
        copy.start()
        pending.append(copy)
        return copy

    def order(chunk):
        return ("x", "y") if chunk % 2 == 0 else ("y", "x")

    def place(axes, fixed):
        return tuple(fixed.get(axis, slice(None)) for axis in axes)

    def scatter_start(buffer, axes, chunk, stage, done, axis, landing, sends, recvs):
        copies = []
        others = [a for a in axes if a not in done and a != axis]
        for ahead in range(1, sizes[axis]):
            device, value = peer(axis, ahead)
            fixed = {a: coords[a] for a in done}
            fixed[axis] = value
            window = tuple(pl.ds(0, sizes[a]) for a in others)
            copies.append(
                remote(
                    buffer.at[(chunk,) + place(axes, fixed)],
                    landing.at[(chunk, ahead - 1) + window],
                    sends.at[chunk, stage, ahead - 1],
                    recvs.at[chunk, stage, ahead - 1],
                    device,
                )
            )
        return copies

    def block_ids(axes):
        ids = [()]
        for axis in axes:
            ids = [i + (j,) for i in ids for j in range(sizes[axis])]
        return ids

    def scatter_end(buffer, axes, chunk, done, axis, landing, copies):
        for copy in copies:
            copy.wait_recv()
        others = [a for a in axes if a not in done and a != axis]
        for ids in block_ids(others):
            fixed = {a: coords[a] for a in done}
            fixed[axis] = coords[axis]
            fixed.update(zip(others, ids))
            at = (chunk,) + place(axes, fixed)
            total = buffer[at].astype(jnp.float32)
            for slot in range(sizes[axis] - 1):
                total = total + landing[(chunk, slot) + ids].astype(jnp.float32)
            if others:
                buffer[at] = total.astype(buffer.dtype)
        return total

    def gather_start(buffer, slot, stage, done, axis):
        fixed = {a: coords[a] for a in ("c", "z", "y", "x") if a not in done}
        copies = []
        prefix = () if slot == chunks else (slot,)
        view = buffer.at[prefix + place(("c", "z", "y", "x"), fixed)]
        for ahead in range(1, sizes[axis]):
            device, _ = peer(axis, ahead)
            copies.append(
                remote(
                    view,
                    view,
                    tok_send.at[slot, stage, ahead - 1],
                    tok_recv.at[slot, stage, ahead - 1],
                    device,
                )
            )
        return copies

    flying = {}
    here = (coords["c"], coords["z"], coords["y"], coords["x"])
    weights[here] = weigh_ref[...]
    weigh_axes = ("z", "y", "x", "c")

    def weigh_step(stage):
        if stage > 0:
            for copy in flying["w", stage - 1]:
                copy.wait_recv()
        if stage < 4:
            flying["w", stage] = gather_start(
                weights, chunks, stage, weigh_axes[:stage], weigh_axes[stage]
            )

    grid_axes = ("z", "y", "x")
    mix_landing = (mix_one, mix_two, mix_last)

    def mix_axis(chunk, stage):
        return (order(chunk) + ("z",))[stage]

    def mix_start(chunk, stage):
        done = (order(chunk) + ("z",))[:stage]
        flying["m", chunk, stage] = scatter_start(
            term, grid_axes, chunk, stage, done, mix_axis(chunk, stage),
            mix_landing[stage], mix_send, mix_recv,
        )

    def mix_end(chunk, stage):
        done = (order(chunk) + ("z",))[:stage]
        return scatter_end(
            term, grid_axes, chunk, done, mix_axis(chunk, stage),
            mix_landing[stage], flying["m", chunk, stage],
        )

    attended = attended_ref[...]
    squares = jnp.zeros((rows, 1), jnp.float32)
    for step in range(chunks + 3):
        if step < chunks:
            span = pl.ds(step * cols, cols)
            term[step] = (
                jnp.dot(attended, proj_ref[:, span], preferred_element_type=jnp.float32)
                .astype(jnp.bfloat16)
                .reshape(term.shape[1:])
            )
            mix_start(step, 0)
        for stage in (1, 2):
            chunk = step - stage
            if 0 <= chunk < chunks:
                mix_end(chunk, stage - 1)
                mix_start(chunk, stage)
        chunk = step - 3
        if 0 <= chunk < chunks:
            span = pl.ds(chunk * cols, cols)
            value = residual_ref[:, span].astype(jnp.float32) + mix_end(chunk, 2)
            stream[:, span] = value
            squares = squares + jnp.sum(value * value, axis=1, keepdims=True)
        if step < 4:
            weigh_step(step)
    inverse = lax.rsqrt(squares / width + norm_eps)

    def gather_axes(chunk):
        first, second = order(chunk)
        return ("z", second, first, "c")

    def token_start(chunk, stage):
        axes = gather_axes(chunk)
        flying["t", chunk, stage] = gather_start(tokens, chunk, stage, axes[:stage], axes[stage])

    for chunk in range(chunks):
        span = pl.ds(chunk * cols, cols)
        tokens[(chunk,) + here] = (stream[:, span] * inverse * gain_ref[:, span]).astype(
            jnp.bfloat16
        )
        token_start(chunk, 0)
    loads[0].wait()
    loads[1].wait()
    group_rows = gate.shape[1]
    for step in range(1, chunks + 4):
        for stage in (1, 2, 3):
            chunk = step - stage
            if 0 <= chunk < chunks:
                for copy in flying["t", chunk, stage - 1]:
                    copy.wait_recv()
                token_start(chunk, stage)
        chunk = step - 4
        if 0 <= chunk < chunks:
            for copy in flying["t", chunk, 3]:
                copy.wait_recv()
            span = pl.ds(chunk * cols, cols)

            def grow(group, carry, chunk=chunk, span=span):
                piece = tokens[chunk, group].reshape(group_rows, cols)
                more_gate = jnp.dot(piece, gate_w[span, :], preferred_element_type=jnp.float32)
                more_upper = jnp.dot(piece, up_w[span, :], preferred_element_type=jnp.float32)
                if chunk > 0:
                    more_gate = gate[group] + more_gate
                    more_upper = upper[group] + more_upper
                if chunk < chunks - 1:
                    gate[group] = more_gate
                    upper[group] = more_upper
                else:
                    act[group] = (jax.nn.silu(more_gate) * more_upper).astype(jnp.bfloat16)
                return carry

            lax.fori_loop(0, sizes["c"], grow, 0)

    weigh_step(4)
    loads[2].wait()

    all_axes = ("c", "z", "y", "x")
    sum_landing = (sum_ctx, sum_one, sum_two, sum_last)

    def sum_axes(chunk):
        return ("c",) + order(chunk) + ("z",)

    def sum_start(chunk, stage):
        axes = sum_axes(chunk)
        flying["s", chunk, stage] = scatter_start(
            parts, all_axes, chunk, stage, axes[:stage], axes[stage],
            sum_landing[stage], sum_send, sum_recv,
        )

    def sum_end(chunk, stage):
        axes = sum_axes(chunk)
        return scatter_end(
            parts, all_axes, chunk, axes[:stage], axes[stage],
            sum_landing[stage], flying["s", chunk, stage],
        )

    lane = lax.broadcasted_iota(jnp.int32, (group_rows, LANES), 1)
    for step in range(chunks + 4):
        if step < chunks:
            span = pl.ds(step * cols, cols)

            def project(ahead, carry, step=step, span=span):
                group = lax.rem(coords["c"] + ahead, sizes["c"])
                held = weights[group].reshape(group_rows, LANES)
                scale = jnp.sum(jnp.where(lane == where_exp, held, 0.0), axis=1, keepdims=True)
                value = jnp.dot(act[group], down_w[:, span], preferred_element_type=jnp.float32)
                parts[step, group] = (
                    (value * scale).astype(jnp.bfloat16).reshape(parts.shape[2:])
                )
                return carry

            lax.fori_loop(0, sizes["c"], project, 0)
            sum_start(step, 0)
        for stage in (1, 2, 3):
            chunk = step - stage
            if 0 <= chunk < chunks:
                sum_end(chunk, stage - 1)
                sum_start(chunk, stage)
        chunk = step - 4
        if 0 <= chunk < chunks:
            span = pl.ds(chunk * cols, cols)
            out_ref[:, span] = (stream[:, span] + sum_end(chunk, 3)).astype(jnp.bfloat16)
    for copy in pending:
        copy.wait_send()


def layer_scratch(sizes, rows, width, hidden):
    contexts, slow, mid, fast = (sizes[axis] for axis in ("c", "z", "y", "x"))
    cols = width // CHUNKS
    wide = max(mid, fast)
    most = max(contexts, slow, wide) - 1
    group = slow * mid * fast * rows
    half, full = jnp.bfloat16, jnp.float32
    one = (CHUNKS, wide - 1, slow, wide, rows, cols)
    two = (CHUNKS, wide - 1, slow, rows, cols)
    last = (CHUNKS, slow - 1, rows, cols)
    grid = (slow, mid, fast, rows)
    buffers = [
        ((CHUNKS,) + grid + (cols,), half),
        (one, half),
        (two, half),
        (last, half),
        ((rows, width), full),
        ((CHUNKS, contexts) + grid + (cols,), half),
        ((contexts,) + grid + (LANES,), full),
        ((width, hidden), half),
        ((width, hidden), half),
        ((hidden, width), half),
        ((contexts, group, hidden), full),
        ((contexts, group, hidden), full),
        ((contexts, group, hidden), half),
        ((CHUNKS, contexts) + grid + (cols,), half),
        ((CHUNKS, contexts - 1) + grid + (cols,), half),
        (one, half),
        (two, half),
        (last, half),
    ]
    size = sum(math.prod(shape) * (2 if kind == half else 4) for shape, kind in buffers)
    semaphores = [
        pltpu.SemaphoreType.DMA((CHUNKS, 3, most)),
        pltpu.SemaphoreType.DMA((CHUNKS, 3, most)),
        pltpu.SemaphoreType.DMA((CHUNKS + 1, 4, most)),
        pltpu.SemaphoreType.DMA((CHUNKS + 1, 4, most)),
        pltpu.SemaphoreType.DMA((CHUNKS, 4, most)),
        pltpu.SemaphoreType.DMA((CHUNKS, 4, most)),
        pltpu.SemaphoreType.DMA((3,)),
    ]
    return [pltpu.VMEM(shape, kind) for shape, kind in buffers] + semaphores, size


def layer_sizes():
    slow, mid, fast = exp_grid(lax.axis_size("exp"))
    return {"c": lax.axis_size("ctx"), "z": slow, "y": mid, "x": fast}


def fused_layer(attended, out_proj, residual, norm_gain, routes, combine, w_gate, w_up, w_down):
    sizes = layer_sizes()
    rows, width = residual.shape
    scratch, _ = layer_scratch(sizes, rows, width, w_gate.shape[2])
    named = routes[:, :, None] == jnp.arange(LANES)[None, None, :]
    weigh = jnp.sum(jnp.where(named, combine[:, :, None], 0.0), axis=1)
    in_vmem = pl.BlockSpec(memory_space=pltpu.VMEM)
    anywhere = pl.BlockSpec(memory_space=pl.ANY)
    return pl.pallas_call(
        functools.partial(layer_kernel, sizes),
        out_shape=jax.ShapeDtypeStruct((rows, width), jnp.bfloat16),
        in_specs=[in_vmem] * 5 + [anywhere] * 3,
        out_specs=in_vmem,
        scratch_shapes=scratch,
        compiler_params=pltpu.CompilerParams(
            collective_id=0, has_side_effects=True, vmem_limit_bytes=VMEM_BUDGET
        ),
    )(
        attended,
        out_proj,
        residual,
        norm_gain.reshape(1, width),
        weigh,
        w_gate[0],
        w_up[0],
        w_down[0],
    )


def from_behind(shard, axis, by):
    peers = lax.axis_size(axis)
    pairs = [(i, i + by) for i in range(peers) if 0 <= i + by < peers]
    return lax.ppermute(shard, axis, pairs)


def per_device(
    queries, keys, values, out_proj, residual, norm_gain, routes, combine, w_gate, w_up, w_down
):
    query_rows = queries.shape[0]
    head_count = queries.shape[1] // HD
    scaling = 1.0 / math.sqrt(HD)
    ctx_where = lax.axis_index("ctx")
    ctx_count = lax.axis_size("ctx")

    def attend(carried, query_heads, pair_block, visible):
        key_count = pair_block.shape[1]
        key_heads = pair_block[0].reshape(key_count, head_count, HD)
        value_heads = pair_block[1].reshape(key_count, head_count, HD)
        scores = (
            jnp.einsum("qhd,khd->hqk", query_heads, key_heads, preferred_element_type=jnp.float32)
            * scaling
        )
        scores = jnp.where(visible, scores, masked_score)
        peak_old, total_old, weighted_old = carried
        peak_new = jnp.maximum(peak_old, jnp.max(scores, axis=2))
        expo_block = jnp.exp(scores - peak_new[:, :, None])
        factor = jnp.exp(peak_old - peak_new)
        total_new = total_old * factor + jnp.sum(expo_block, axis=2)
        weighted_new = weighted_old * factor.T[:, :, None] + jnp.einsum(
            "hqk,khd->qhd",
            expo_block.astype(jnp.bfloat16),
            value_heads,
            preferred_element_type=jnp.float32,
        )
        return (peak_new, total_new, weighted_new)

    initial = (
        jnp.full((head_count, query_rows), masked_score, jnp.float32),
        jnp.zeros((head_count, query_rows), jnp.float32),
        jnp.zeros((query_rows, head_count, HD), jnp.float32),
    )
    query_heads = queries.reshape(query_rows, head_count, HD)
    row_ids = jnp.arange(query_rows)
    diag_mask = row_ids[:, None] >= row_ids[None, :]
    pair_block = jnp.stack([keys, values])
    carried = attend(initial, query_heads, pair_block, diag_mask)
    for step_index in range(1, ctx_count):
        pair_block = from_behind(pair_block, "ctx", 1)
        carried = attend(carried, query_heads, pair_block, ctx_where >= step_index)
    attended = (
        (carried[2] / carried[1].T[:, :, None])
        .astype(jnp.bfloat16)
        .reshape(query_rows, head_count * HD)
    )
    tok_count = residual.shape[0]
    _, scratch_bytes = layer_scratch(
        layer_sizes(), tok_count, residual.shape[1], w_gate.shape[2]
    )
    if scratch_bytes < VMEM_BUDGET - 8 * 1024 * 1024 and lax.axis_size("exp") <= LANES:
        return fused_layer(
            attended, out_proj, residual, norm_gain, routes, combine, w_gate, w_up, w_down
        )
    term = jnp.dot(attended, out_proj, preferred_element_type=jnp.float32)
    mixed = lax.psum_scatter(
        lax.optimization_barrier(term.astype(jnp.bfloat16))
        .astype(jnp.float32)
        .astype(jnp.bfloat16),
        "exp",
        scatter_dimension=0,
        tiled=True,
    ).astype(jnp.float32)
    stream = residual.astype(jnp.float32) + mixed
    normed = (
        stream * lax.rsqrt(jnp.mean(stream * stream, axis=1, keepdims=True) + norm_eps) * norm_gain
    ).astype(jnp.bfloat16)
    width = normed.shape[1]
    per_token = routes.shape[1]
    experts = lax.axis_size("exp")
    capacity = min(tok_count, max(2, tok_count * per_token * 5 // (4 * experts)))
    pair_count = tok_count * per_token
    flat_routes = routes.reshape(pair_count)
    expert_hot = (flat_routes[:, None] == jnp.arange(experts)[None, :]).astype(jnp.float32)
    pair_ids = jnp.arange(pair_count)
    before = (pair_ids[:, None] > pair_ids[None, :]).astype(jnp.float32)
    earlier = jnp.dot(before, expert_hot, preferred_element_type=jnp.float32)
    slot_index = jnp.sum(earlier * expert_hot, axis=1).astype(jnp.int32)
    position = flat_routes * capacity + slot_index
    position_hot = (position[:, None] == jnp.arange(experts * capacity)[None, :]).astype(
        jnp.float32
    )
    token_hot = (
        (jnp.arange(pair_count) // per_token)[:, None] == jnp.arange(tok_count)[None, :]
    ).astype(jnp.float32)
    pick_rows = jnp.einsum("pr,pt->rt", position_hot, token_hot).astype(jnp.bfloat16)
    outgoing = (
        jnp.dot(pick_rows, normed, preferred_element_type=jnp.float32)
        .astype(jnp.bfloat16)
        .reshape(experts, capacity, width)
    )
    received = lax.all_to_all(outgoing, "exp", split_axis=0, concat_axis=0, tiled=True)
    gate_local = w_gate[0]
    up_local = w_up[0]
    down_local = w_down[0]
    piece = lax.all_gather(received, "ctx", axis=0, tiled=True)
    gate = jnp.einsum("smd,df->smf", piece, gate_local, preferred_element_type=jnp.float32)
    upper = jnp.einsum("smd,df->smf", piece, up_local, preferred_element_type=jnp.float32)
    act_all = (jax.nn.silu(gate) * upper).astype(jnp.bfloat16)
    expert_out = lax.psum_scatter(
        jnp.einsum("smf,fd->smd", act_all, down_local, preferred_element_type=jnp.float32).astype(
            jnp.bfloat16
        ),
        "ctx",
        scatter_dimension=0,
        tiled=True,
    )
    returned = lax.all_to_all(expert_out, "exp", split_axis=0, concat_axis=0, tiled=True)
    weigh_rows = jnp.einsum(
        "pr,pt->tr", position_hot, token_hot * combine.reshape(pair_count)[:, None]
    )
    moe_sum = jnp.dot(
        weigh_rows,
        returned.reshape(experts * capacity, width).astype(jnp.float32),
        precision=lax.Precision.HIGHEST,
    )
    return (stream + moe_sum).astype(jnp.bfloat16)


def solution(mesh):
    in_specs = (
        P("ctx", "exp"),
        P("ctx", "exp"),
        P("ctx", "exp"),
        P("exp", None),
        P(("ctx", "exp"), None),
        P(),
        P(("ctx", "exp"), None),
        P(("ctx", "exp"), None),
        P("exp", None, "ctx"),
        P("exp", None, "ctx"),
        P("exp", "ctx", None),
    )
    out_specs = P(("ctx", "exp"), None)
    return jax.shard_map(
        per_device, mesh=mesh, in_specs=in_specs, out_specs=out_specs, check_vma=False
    )
```

```python
import functools
import math

import jax
import jax.numpy as jnp
from jax import lax
from jax.experimental import pallas as pl
from jax.experimental.pallas import tpu as pltpu
from jax.sharding import PartitionSpec as P

HD = 128
LANES = 128
CHUNKS = 7
MIX_STEPS = (0, 2, 3, 4, 5, 6, 8, 9)
SUM_STEPS = (0, 1, 3, 4, 5)
VMEM_BUDGET = 58 * 1024 * 1024


masked_score = -1e30
norm_eps = 1e-06


def exp_grid(experts):
    fast = 2 if experts % 2 == 0 else 1
    slow = 4 if (experts // fast) % 4 == 0 else 1
    return slow, experts // (fast * slow), fast


def layer_kernel(
    sizes,
    attended_ref,
    proj_ref,
    residual_ref,
    gain_ref,
    weigh_ref,
    gate_hbm,
    up_hbm,
    down_hbm,
    out_ref,
    term,
    mix_one,
    mix_two,
    mix_last,
    stream,
    tokens,
    weights,
    gate_w,
    up_w,
    down_w,
    gate,
    upper,
    act,
    parts,
    sum_ctx,
    sum_one,
    sum_two,
    sum_last,
    mix_send,
    mix_recv,
    tok_send,
    tok_recv,
    sum_send,
    sum_recv,
    load_sem,
):
    rows, width = residual_ref.shape
    chunks = term.shape[0]
    cols = width // chunks
    where_exp = lax.axis_index("exp")
    block = sizes["y"] * sizes["x"]
    coords = {
        "c": lax.axis_index("ctx"),
        "z": lax.div(where_exp, block),
        "y": lax.rem(lax.div(where_exp, sizes["x"]), sizes["y"]),
        "x": lax.rem(where_exp, sizes["x"]),
    }

    def peer(axis, ahead):
        there = dict(coords)
        there[axis] = lax.rem(coords[axis] + ahead, sizes[axis])
        number = (there["z"] * sizes["y"] + there["y"]) * sizes["x"] + there["x"]
        return (there["c"], number), there[axis]

    loads = [
        pltpu.make_async_copy(source, target, load_sem.at[i])
        for i, (source, target) in enumerate(
            ((gate_hbm, gate_w), (up_hbm, up_w), (down_hbm, down_w))
        )
    ]
    for load in loads:
        load.start()

    barrier = pltpu.get_barrier_semaphore()
    greeted = 0
    for axis in ("c", "z", "y", "x"):
        for ahead in range(1, sizes[axis]):
            device, _ = peer(axis, ahead)
            pl.semaphore_signal(
                barrier, inc=1, device_id=device, device_id_type=pl.DeviceIdType.MESH
            )
            greeted += 1
    pl.semaphore_wait(barrier, greeted)

    pending = []

    def remote(source, target, send_sem, recv_sem, device):
        copy = pltpu.make_async_remote_copy(
            src_ref=source,
            dst_ref=target,
            send_sem=send_sem,
            recv_sem=recv_sem,
            device_id=device,
            device_id_type=pl.DeviceIdType.MESH,
        )
        copy.start()
        pending.append(copy)
        return copy

    def order(chunk):
        return ("x", "y") if chunk % 2 == 0 else ("y", "x")

    def place(axes, fixed):
        return tuple(fixed.get(axis, slice(None)) for axis in axes)

    def scatter_start(buffer, axes, chunk, stage, done, axis, landing, sends, recvs):
        copies = []
        others = [a for a in axes if a not in done and a != axis]
        for ahead in range(1, sizes[axis]):
            device, value = peer(axis, ahead)
            fixed = {a: coords[a] for a in done}
            fixed[axis] = value
            window = tuple(pl.ds(0, sizes[a]) for a in others)
            copies.append(
                remote(
                    buffer.at[(chunk,) + place(axes, fixed)],
                    landing.at[(chunk, ahead - 1) + window],
                    sends.at[chunk, stage, ahead - 1],
                    recvs.at[chunk, stage, ahead - 1],
                    device,
                )
            )
        return copies

    def block_ids(axes):
        ids = [()]
        for axis in axes:
            ids = [i + (j,) for i in ids for j in range(sizes[axis])]
        return ids

    def scatter_end(buffer, axes, chunk, done, axis, landing, copies):
        for copy in copies:
            copy.wait_recv()
        others = [a for a in axes if a not in done and a != axis]
        for ids in block_ids(others):
            fixed = {a: coords[a] for a in done}
            fixed[axis] = coords[axis]
            fixed.update(zip(others, ids))
            at = (chunk,) + place(axes, fixed)
            total = buffer[at].astype(jnp.float32)
            for slot in range(sizes[axis] - 1):
                total = total + landing[(chunk, slot) + ids].astype(jnp.float32)
            if others:
                buffer[at] = total.astype(buffer.dtype)
        return total

    def gather_start(buffer, slot, stage, done, axis):
        fixed = {a: coords[a] for a in ("c", "z", "y", "x") if a not in done}
        copies = []
        prefix = () if slot == chunks else (slot,)
        view = buffer.at[prefix + place(("c", "z", "y", "x"), fixed)]
        for ahead in range(1, sizes[axis]):
            device, _ = peer(axis, ahead)
            copies.append(
                remote(
                    view,
                    view,
                    tok_send.at[slot, stage, ahead - 1],
                    tok_recv.at[slot, stage, ahead - 1],
                    device,
                )
            )
        return copies

    flying = {}
    here = (coords["c"], coords["z"], coords["y"], coords["x"])
    weigh_axes = ("z", "y", "x", "c")

    def weigh_step(stage):
        if stage > 0:
            for copy in flying["w", stage - 1]:
                copy.wait_recv()
        if stage < 4:
            flying["w", stage] = gather_start(
                weights, chunks, stage, weigh_axes[:stage], weigh_axes[stage]
            )

    grid_axes = ("z", "y", "x")
    mix_landing = (mix_one, mix_two, mix_last)

    def mix_axis(chunk, stage):
        return (order(chunk) + ("z",))[stage]

    def mix_start(chunk, stage):
        done = (order(chunk) + ("z",))[:stage]
        flying["m", chunk, stage] = scatter_start(
            term, grid_axes, chunk, stage, done, mix_axis(chunk, stage),
            mix_landing[stage], mix_send, mix_recv,
        )

    def mix_end(chunk, stage):
        done = (order(chunk) + ("z",))[:stage]
        return scatter_end(
            term, grid_axes, chunk, done, mix_axis(chunk, stage),
            mix_landing[stage], flying["m", chunk, stage],
        )

    def gather_axes(chunk):
        first, second = order(chunk)
        return ("z", second, first, "c")

    def token_start(chunk, stage):
        axes = gather_axes(chunk)
        flying["t", chunk, stage] = gather_start(tokens, chunk, stage, axes[:stage], axes[stage])

    attended = attended_ref[...]
    squares = jnp.zeros((rows, 1), jnp.float32)
    group_rows = gate.shape[1]
    lane = lax.broadcasted_iota(jnp.int32, (group_rows, LANES), 1)

    def pick(group, number):
        held = weights[group].reshape(group_rows, LANES)
        return jnp.sum(jnp.where(lane == number, held, 0.0), axis=1, keepdims=True)

    def advance(chunk, stage, squares):
        span = pl.ds(chunk * cols, cols)
        newest = chunk == chunks - 1
        if stage == 0:
            term[chunk] = (
                jnp.dot(attended, proj_ref[:, span], preferred_element_type=jnp.float32)
                .astype(jnp.bfloat16)
                .reshape(term.shape[1:])
            )
            mix_start(chunk, 0)
        elif stage < 3:
            mix_end(chunk, stage - 1)
            mix_start(chunk, stage)
        elif stage == 3:
            value = residual_ref[:, span].astype(jnp.float32) + mix_end(chunk, 2)
            stream[:, span] = value
            squares = squares + jnp.sum(value * value, axis=1, keepdims=True)
            if newest:
                inverse = lax.rsqrt(squares / width + norm_eps)
                own_lane = lax.broadcasted_iota(jnp.int32, (rows, LANES), 1)
                weights[here] = jnp.where(own_lane == LANES - 1, inverse, weigh_ref[...])
                weigh_step(0)
            tokens[(chunk,) + here] = (value * gain_ref[:, span]).astype(jnp.bfloat16)
            token_start(chunk, 0)
        else:
            if newest:
                weigh_step(stage - 3)
            for copy in flying["t", chunk, stage - 4]:
                copy.wait_recv()
            if stage < 7:
                token_start(chunk, stage - 3)
                return squares
            if chunk == 0:
                loads[0].wait()
                loads[1].wait()

            def grow(group, carry):
                piece = tokens[chunk, group].reshape(group_rows, cols)
                more_gate = jnp.dot(piece, gate_w[span, :], preferred_element_type=jnp.float32)
                more_upper = jnp.dot(piece, up_w[span, :], preferred_element_type=jnp.float32)
                if chunk > 0:
                    more_gate = gate[group] + more_gate
                    more_upper = upper[group] + more_upper
                if chunk < chunks - 1:
                    gate[group] = more_gate
                    upper[group] = more_upper
                else:
                    inverse = pick(group, LANES - 1)
                    act[group] = (
                        jax.nn.silu(more_gate * inverse) * (more_upper * inverse)
                    ).astype(jnp.bfloat16)
                return carry

            lax.fori_loop(0, sizes["c"], grow, 0)
        return squares

    for step in range(chunks + MIX_STEPS[-1]):
        for stage, delay in enumerate(MIX_STEPS):
            if 0 <= step - delay < chunks:
                squares = advance(step - delay, stage, squares)
    loads[2].wait()

    all_axes = ("c", "z", "y", "x")
    sum_landing = (sum_ctx, sum_one, sum_two, sum_last)

    def sum_axes(chunk):
        return ("c",) + order(chunk) + ("z",)

    def sum_start(chunk, stage):
        axes = sum_axes(chunk)
        flying["s", chunk, stage] = scatter_start(
            parts, all_axes, chunk, stage, axes[:stage], axes[stage],
            sum_landing[stage], sum_send, sum_recv,
        )

    def sum_end(chunk, stage):
        axes = sum_axes(chunk)
        return scatter_end(
            parts, all_axes, chunk, axes[:stage], axes[stage],
            sum_landing[stage], flying["s", chunk, stage],
        )

    for step in range(chunks + SUM_STEPS[-1]):
        if step < chunks:
            span = pl.ds(step * cols, cols)

            def project(ahead, carry, step=step, span=span):
                group = lax.rem(coords["c"] + ahead, sizes["c"])
                scale = pick(group, where_exp)
                value = jnp.dot(act[group], down_w[:, span], preferred_element_type=jnp.float32)
                parts[step, group] = (
                    (value * scale).astype(jnp.bfloat16).reshape(parts.shape[2:])
                )
                return carry

            lax.fori_loop(0, sizes["c"], project, 0)
            sum_start(step, 0)
        for stage in (1, 2, 3):
            chunk = step - SUM_STEPS[stage]
            if 0 <= chunk < chunks:
                sum_end(chunk, stage - 1)
                sum_start(chunk, stage)
        chunk = step - SUM_STEPS[4]
        if 0 <= chunk < chunks:
            span = pl.ds(chunk * cols, cols)
            out_ref[:, span] = (stream[:, span] + sum_end(chunk, 3)).astype(jnp.bfloat16)
    for copy in pending:
        copy.wait_send()


def layer_scratch(sizes, rows, width, hidden):
    contexts, slow, mid, fast = (sizes[axis] for axis in ("c", "z", "y", "x"))
    cols = width // CHUNKS
    wide = max(mid, fast)
    most = max(contexts, slow, wide) - 1
    group = slow * mid * fast * rows
    half, full = jnp.bfloat16, jnp.float32
    one = (CHUNKS, wide - 1, slow, wide, rows, cols)
    two = (CHUNKS, wide - 1, slow, rows, cols)
    last = (CHUNKS, slow - 1, rows, cols)
    grid = (slow, mid, fast, rows)
    buffers = [
        ((CHUNKS,) + grid + (cols,), half),
        (one, half),
        (two, half),
        (last, half),
        ((rows, width), full),
        ((CHUNKS, contexts) + grid + (cols,), half),
        ((contexts,) + grid + (LANES,), full),
        ((width, hidden), half),
        ((width, hidden), half),
        ((hidden, width), half),
        ((contexts, group, hidden), full),
        ((contexts, group, hidden), full),
        ((contexts, group, hidden), half),
        ((CHUNKS, contexts) + grid + (cols,), half),
        ((CHUNKS, contexts - 1) + grid + (cols,), half),
        (one, half),
        (two, half),
        (last, half),
    ]
    size = sum(math.prod(shape) * (2 if kind == half else 4) for shape, kind in buffers)
    semaphores = [
        pltpu.SemaphoreType.DMA((CHUNKS, 3, most)),
        pltpu.SemaphoreType.DMA((CHUNKS, 3, most)),
        pltpu.SemaphoreType.DMA((CHUNKS + 1, 4, most)),
        pltpu.SemaphoreType.DMA((CHUNKS + 1, 4, most)),
        pltpu.SemaphoreType.DMA((CHUNKS, 4, most)),
        pltpu.SemaphoreType.DMA((CHUNKS, 4, most)),
        pltpu.SemaphoreType.DMA((3,)),
    ]
    return [pltpu.VMEM(shape, kind) for shape, kind in buffers] + semaphores, size


def layer_sizes():
    slow, mid, fast = exp_grid(lax.axis_size("exp"))
    return {"c": lax.axis_size("ctx"), "z": slow, "y": mid, "x": fast}


def fused_layer(attended, out_proj, residual, norm_gain, routes, combine, w_gate, w_up, w_down):
    sizes = layer_sizes()
    rows, width = residual.shape
    scratch, _ = layer_scratch(sizes, rows, width, w_gate.shape[2])
    named = routes[:, :, None] == jnp.arange(LANES)[None, None, :]
    weigh = jnp.sum(jnp.where(named, combine[:, :, None], 0.0), axis=1)
    in_vmem = pl.BlockSpec(memory_space=pltpu.VMEM)
    anywhere = pl.BlockSpec(memory_space=pl.ANY)
    return pl.pallas_call(
        functools.partial(layer_kernel, sizes),
        out_shape=jax.ShapeDtypeStruct((rows, width), jnp.bfloat16),
        in_specs=[in_vmem] * 5 + [anywhere] * 3,
        out_specs=in_vmem,
        scratch_shapes=scratch,
        compiler_params=pltpu.CompilerParams(
            collective_id=0, has_side_effects=True, vmem_limit_bytes=VMEM_BUDGET
        ),
    )(
        attended,
        out_proj,
        residual,
        norm_gain.reshape(1, width),
        weigh,
        w_gate[0],
        w_up[0],
        w_down[0],
    )


def from_behind(shard, axis, by):
    peers = lax.axis_size(axis)
    pairs = [(i, i + by) for i in range(peers) if 0 <= i + by < peers]
    return lax.ppermute(shard, axis, pairs)


def per_device(
    queries, keys, values, out_proj, residual, norm_gain, routes, combine, w_gate, w_up, w_down
):
    query_rows = queries.shape[0]
    head_count = queries.shape[1] // HD
    scaling = 1.0 / math.sqrt(HD)
    ctx_where = lax.axis_index("ctx")
    ctx_count = lax.axis_size("ctx")

    def attend(carried, query_heads, pair_block, visible):
        key_count = pair_block.shape[1]
        key_heads = pair_block[0].reshape(key_count, head_count, HD)
        value_heads = pair_block[1].reshape(key_count, head_count, HD)
        scores = (
            jnp.einsum("qhd,khd->hqk", query_heads, key_heads, preferred_element_type=jnp.float32)
            * scaling
        )
        scores = jnp.where(visible, scores, masked_score)
        peak_old, total_old, weighted_old = carried
        peak_new = jnp.maximum(peak_old, jnp.max(scores, axis=2))
        expo_block = jnp.exp(scores - peak_new[:, :, None])
        factor = jnp.exp(peak_old - peak_new)
        total_new = total_old * factor + jnp.sum(expo_block, axis=2)
        weighted_new = weighted_old * factor.T[:, :, None] + jnp.einsum(
            "hqk,khd->qhd",
            expo_block.astype(jnp.bfloat16),
            value_heads,
            preferred_element_type=jnp.float32,
        )
        return (peak_new, total_new, weighted_new)

    initial = (
        jnp.full((head_count, query_rows), masked_score, jnp.float32),
        jnp.zeros((head_count, query_rows), jnp.float32),
        jnp.zeros((query_rows, head_count, HD), jnp.float32),
    )
    query_heads = queries.reshape(query_rows, head_count, HD)
    row_ids = jnp.arange(query_rows)
    diag_mask = row_ids[:, None] >= row_ids[None, :]
    pair_block = jnp.stack([keys, values])
    carried = attend(initial, query_heads, pair_block, diag_mask)
    for step_index in range(1, ctx_count):
        pair_block = from_behind(pair_block, "ctx", 1)
        carried = attend(carried, query_heads, pair_block, ctx_where >= step_index)
    attended = (
        (carried[2] / carried[1].T[:, :, None])
        .astype(jnp.bfloat16)
        .reshape(query_rows, head_count * HD)
    )
    tok_count = residual.shape[0]
    _, scratch_bytes = layer_scratch(
        layer_sizes(), tok_count, residual.shape[1], w_gate.shape[2]
    )
    if scratch_bytes < VMEM_BUDGET - 8 * 1024 * 1024 and lax.axis_size("exp") < LANES:
        return fused_layer(
            attended, out_proj, residual, norm_gain, routes, combine, w_gate, w_up, w_down
        )
    term = jnp.dot(attended, out_proj, preferred_element_type=jnp.float32)
    mixed = lax.psum_scatter(
        lax.optimization_barrier(term.astype(jnp.bfloat16))
        .astype(jnp.float32)
        .astype(jnp.bfloat16),
        "exp",
        scatter_dimension=0,
        tiled=True,
    ).astype(jnp.float32)
    stream = residual.astype(jnp.float32) + mixed
    normed = (
        stream * lax.rsqrt(jnp.mean(stream * stream, axis=1, keepdims=True) + norm_eps) * norm_gain
    ).astype(jnp.bfloat16)
    width = normed.shape[1]
    per_token = routes.shape[1]
    experts = lax.axis_size("exp")
    capacity = min(tok_count, max(2, tok_count * per_token * 5 // (4 * experts)))
    pair_count = tok_count * per_token
    flat_routes = routes.reshape(pair_count)
    expert_hot = (flat_routes[:, None] == jnp.arange(experts)[None, :]).astype(jnp.float32)
    pair_ids = jnp.arange(pair_count)
    before = (pair_ids[:, None] > pair_ids[None, :]).astype(jnp.float32)
    earlier = jnp.dot(before, expert_hot, preferred_element_type=jnp.float32)
    slot_index = jnp.sum(earlier * expert_hot, axis=1).astype(jnp.int32)
    position = flat_routes * capacity + slot_index
    position_hot = (position[:, None] == jnp.arange(experts * capacity)[None, :]).astype(
        jnp.float32
    )
    token_hot = (
        (jnp.arange(pair_count) // per_token)[:, None] == jnp.arange(tok_count)[None, :]
    ).astype(jnp.float32)
    pick_rows = jnp.einsum("pr,pt->rt", position_hot, token_hot).astype(jnp.bfloat16)
    outgoing = (
        jnp.dot(pick_rows, normed, preferred_element_type=jnp.float32)
        .astype(jnp.bfloat16)
        .reshape(experts, capacity, width)
    )
    received = lax.all_to_all(outgoing, "exp", split_axis=0, concat_axis=0, tiled=True)
    gate_local = w_gate[0]
    up_local = w_up[0]
    down_local = w_down[0]
    piece = lax.all_gather(received, "ctx", axis=0, tiled=True)
    gate = jnp.einsum("smd,df->smf", piece, gate_local, preferred_element_type=jnp.float32)
    upper = jnp.einsum("smd,df->smf", piece, up_local, preferred_element_type=jnp.float32)
    act_all = (jax.nn.silu(gate) * upper).astype(jnp.bfloat16)
    expert_out = lax.psum_scatter(
        jnp.einsum("smf,fd->smd", act_all, down_local, preferred_element_type=jnp.float32).astype(
            jnp.bfloat16
        ),
        "ctx",
        scatter_dimension=0,
        tiled=True,
    )
    returned = lax.all_to_all(expert_out, "exp", split_axis=0, concat_axis=0, tiled=True)
    weigh_rows = jnp.einsum(
        "pr,pt->tr", position_hot, token_hot * combine.reshape(pair_count)[:, None]
    )
    moe_sum = jnp.dot(
        weigh_rows,
        returned.reshape(experts * capacity, width).astype(jnp.float32),
        precision=lax.Precision.HIGHEST,
    )
    return (stream + moe_sum).astype(jnp.bfloat16)


def solution(mesh):
    in_specs = (
        P("ctx", "exp"),
        P("ctx", "exp"),
        P("ctx", "exp"),
        P("exp", None),
        P(("ctx", "exp"), None),
        P(),
        P(("ctx", "exp"), None),
        P(("ctx", "exp"), None),
        P("exp", None, "ctx"),
        P("exp", None, "ctx"),
        P("exp", "ctx", None),
    )
    out_specs = P(("ctx", "exp"), None)
    return jax.shard_map(
        per_device, mesh=mesh, in_specs=in_specs, out_specs=out_specs, check_vma=False
    )
```
